256 devices in a mesh: hst: 32 (over z_lo, x, core), kv: 8 (over z_hi, y).
Axes of the slice: x: 4, y: 4, z: 8 (z_hi: 2, z_lo: 4; z = z_hi * 4 + z_lo), core: 2. Of those that a mesh axis runs over, the one named last changes fastest.
Arguments:
- queries: bfloat16 [16384, 4096], P('hst', 'kv'), may hold values from -160 to 160
- keys: bfloat16 [16384, 1024], P('hst', 'kv'), may hold values from -4 to 4
- values: bfloat16 [16384, 1024], P('hst', 'kv'), may hold values from -4 to 4
- out_weight: bfloat16 [4096, 4096], P('kv'), may hold values from -0.09375 to 0.09375
- keep: int32 [32, 8, 256], P('hst', 'kv'), may hold values from 0 to 511, as said below
- anchor_len: int32 [8], P('kv'), may hold values from 64 to 256, as said below
Outputs:
- projected: bfloat16 [16384, 4096], P(('hst', 'kv'))
The draws below stay inside these ranges and needn't reach their ends.
Inputs may be any that keep to these rules, and one draw needn't show every extreme that they name: `keep`: within one block and KV head the 256 positions are distinct. `anchor_len`: at least one KV head has 256 live anchor rows.
All inputs are finite; a program needn't handle non-finite values.
Results may differ from the reference program's by a relative error of at most 0.018.
Values may be sent and summed in bfloat16 or wider, within the bound.
A program may use at most 64 MiB of HBM per device.

```python
import math
import jax
import jax.numpy as jnp
from jax import lax

D = 4096
HD = 128
QPG = 4
BLK = 512
KVH = 8
HEADS = 32
KEEP = 256
ANC = 256
HOSTS = 32
TOKENS = 16384
N_HST = 32


def paired_keys(key):
    key = jax.random.fold_in(key, 11)
    base = jnp.clip(jax.random.normal(key, (TOKENS, KVH * HD), jnp.float32), -4.0, 4.0)
    return base


def draw_keys(key, part):
    return paired_keys(key).astype(jnp.bfloat16)


def draw_queries(key, part):
    key = jax.random.fold_in(key, 5)
    base = jnp.clip(jax.random.normal(key, (TOKENS, HEADS * HD), jnp.float32), -4.0, 4.0)
    return base.astype(jnp.bfloat16)


def draw_anchor_len(key, part):
    key = jax.random.fold_in(key, 7)
    lengths = jax.random.randint(key, (KVH,), ANC // 4, ANC + 1)
    picked = jax.random.randint(jax.random.fold_in(key, 1), (), 0, KVH)
    return jnp.where(jnp.arange(KVH) == picked, ANC, lengths).astype(jnp.int32)


def draw_keep(key, part):
    key = jax.random.fold_in(key, 9)
    subkeys = jax.random.split(key, HOSTS * KVH)
    lists = jax.vmap(lambda subkey: jax.random.permutation(subkey, BLK)[:KEEP])(subkeys)
    return lists.reshape(HOSTS, KVH, KEEP).astype(jnp.int32)


def shard_levels(rng, shape, cuts, least, high):
    def one(axis_at, parts):
        heights = jax.random.uniform(jax.random.fold_in(jax.random.fold_in(rng, 6), axis_at), (parts,), jnp.float32, least / len(cuts), high / len(cuts))
        return jnp.repeat(jnp.exp(heights), shape[axis_at] // parts).reshape((-1,) + (1,) * (len(shape) - axis_at - 1))

    level = one(*cuts[0])
    for cut in cuts[1:]:
        level = level * one(*cut)
    return level


def gaussian(own_key, extent, scale, limit, shards=(), kind=jnp.bfloat16):
    drawn = jax.random.normal(own_key, extent, jnp.float32) * scale
    if len(shards) > 0:
        drawn = shard_levels(own_key, extent, shards, -0.22, 0.18) * drawn
    return jnp.clip(drawn, min=-limit, max=limit).astype(kind)


def setup_inputs(seed: int = 0) -> dict:
    streams_of = jax.random.split(jax.random.key(seed), 7)
    queries = draw_queries(jax.random.fold_in(streams_of[6], 71), 0)
    keys = draw_keys(jax.random.fold_in(streams_of[6], 71), 0)
    values = gaussian(streams_of[2], (TOKENS, KVH * HD), 1.0, 4.0, ((0, 32), (1, 8)))
    out_weight = gaussian(streams_of[3], (HEADS * HD, D), (HEADS * HD) ** -0.5, 0.09375, ((0, 8),))
    keep = draw_keep(jax.random.fold_in(streams_of[6], 71), 0)
    anchor_len = draw_anchor_len(jax.random.fold_in(streams_of[6], 71), 0)
    return dict(queries=queries, keys=keys, values=values, out_weight=out_weight, keep=keep, anchor_len=anchor_len)


def reference(queries, keys, values, out_weight, keep, anchor_len):
    hosts = N_HST
    scale = 1.0 / math.sqrt(HD)
    key_blocks = keys.reshape(hosts, BLK, KVH, HD).transpose(0, 2, 1, 3)
    value_blocks = values.reshape(hosts, BLK, KVH, HD).transpose(0, 2, 1, 3)
    query_blocks = queries.reshape(hosts, BLK, KVH, QPG, HD).transpose(0, 2, 3, 1, 4)
    gather_index = keep[..., None].astype(jnp.int32)
    pass_keys = jnp.take_along_axis(key_blocks, gather_index, axis=2)
    pass_values = jnp.take_along_axis(value_blocks, gather_index, axis=2)
    flat_keys = pass_keys.transpose(1, 0, 2, 3).reshape(KVH, hosts * KEEP, HD)
    flat_values = pass_values.transpose(1, 0, 2, 3).reshape(KVH, hosts * KEEP, HD)
    anchor_keys = key_blocks[0, :, :ANC]
    anchor_values = value_blocks[0, :, :ANC]
    positions = jnp.arange(BLK)
    causal = positions[:, None] >= positions[None, :]
    pass_owner = jnp.arange(hosts * KEEP) // KEEP
    anchor_rows = jnp.arange(ANC)

    def one_group(host_index, query_group, local_keys, local_values, group_anchor_k, group_anchor_v, group_pass_k, group_pass_v, group_len):
        joined_keys = jnp.concatenate([group_anchor_k, group_pass_k, local_keys], 0).astype(jnp.float32)
        joined_values = jnp.concatenate([group_anchor_v, group_pass_v, local_values], 0).astype(jnp.float32)
        anchor_ok = (anchor_rows < group_len) & (host_index > 0)
        pass_ok = pass_owner < host_index
        allowed = jnp.concatenate([jnp.broadcast_to(anchor_ok[None, :], (BLK, ANC)), jnp.broadcast_to(pass_ok[None, :], (BLK, hosts * KEEP)), causal], 1)
        scores = jnp.einsum('hqd,kd->hqk', query_group.astype(jnp.float32), joined_keys) * scale
        scores = jnp.where(allowed[None], scores, -jnp.inf)
        row_max = lax.optimization_barrier(jnp.max(scores, -1, keepdims=True))
        raised = jnp.exp(scores - row_max)
        row_sums = lax.optimization_barrier(jnp.sum(raised, -1))
        probs = lax.optimization_barrier(raised.astype(jnp.bfloat16)).astype(jnp.float32)
        attended_group = jnp.einsum('hqk,kd->hqd', probs, joined_values) / row_sums[..., None]
        return attended_group.astype(jnp.bfloat16)

    def one_host(inputs):
        host_index, query_host, keys_host, values_host = inputs
        return jax.vmap(one_group, in_axes=(None, 0, 0, 0, 0, 0, 0, 0, 0))(host_index, query_host, keys_host, values_host, anchor_keys, anchor_values, flat_keys, flat_values, anchor_len)
    host_ids = jnp.arange(hosts).astype(jnp.int32)
    attended = lax.map(one_host, (host_ids, query_blocks, key_blocks, value_blocks))
    attended = attended.transpose(0, 3, 1, 2, 4).reshape(TOKENS, KVH, QPG * HD)
    weight_groups = out_weight.reshape(KVH, QPG * HD, D)

    def add_group(summed, group_pair):
        part = jnp.dot(group_pair[0], group_pair[1], preferred_element_type=jnp.float32)
        part = lax.optimization_barrier(part.astype(jnp.bfloat16)).astype(jnp.float32)
        return (summed + part, None)
    summed = lax.scan(add_group, jnp.zeros((TOKENS, D), jnp.float32), (attended.transpose(1, 0, 2), weight_groups))[0]
    return summed.astype(jnp.bfloat16)
```

```python
import functools
import math

import jax
import jax.numpy as jnp
from jax import lax
from jax.experimental import pallas as pl
from jax.experimental.pallas import tpu as pltpu
from jax.sharding import PartitionSpec as P

HD = 128
QPG = 4
BLK = 512
KEEP = 256
NX, NZ, NY = 4, 4, 4
PLANE = 2 * NX
NCH = 4
ROWS = BLK // NCH
QROWS = QPG * ROWS
COLS = 1024
SCALE = math.log2(math.e) / math.sqrt(HD)
NEG = -1e30
F32, BF16 = jnp.float32, jnp.bfloat16
MESH = pl.DeviceIdType.MESH


def kernel(
    q_ref, k_ref, v_ref, keep_ref, alen_ref, w_ref, out_ref,
    kvown, kvbuf, qs, m_s, l_s, acc_s, xbuf, wbuf, ysc, yown, ysend, zbuf, fbuf,
    kv_send, kv_recv, w_send, w_recv, wl_send, wl_recv, w_own,
    x_send, x_recv, z_send, z_recv, o_send, o_recv,
):
    h = lax.axis_index("hst")
    g = lax.axis_index("kv")
    z, x, c = h // PLANE, (h % PLANE) // 2, h % 2
    zh, y = g // NY, g % NY
    right = z * PLANE + 2 * ((x + 1) % NX) + c
    left = z * PLANE + 2 * ((x + NX - 1) % NX) + c
    sib = z * PLANE + 2 * x + (1 - c)
    other = (1 - zh) * NY + y

    def at_y(d):
        return zh * NY + (y + d) % NY

    def remote(src, dst, send, recv, device):
        return pltpu.make_async_remote_copy(
            src_ref=src, dst_ref=dst, send_sem=send, recv_sem=recv,
            device_id=device, device_id_type=MESH,
        )

    def start(copy):
        copy.start()

    def sent(copy):
        copy.wait_send()

    barrier = pltpu.get_barrier_semaphore()
    partners = [(right, g), (left, g), (sib, g), (h, other)]
    partners += [(h, at_y(d)) for d in (1, 2, 3)]
    for device in partners:
        pl.semaphore_signal(barrier, inc=1, device_id=device, device_id_type=MESH)

    @pl.when(z < NZ - 1)
    def _():
        pl.semaphore_signal(barrier, inc=1, device_id=(h + PLANE, g), device_id_type=MESH)

    @pl.when(z > 0)
    def _():
        pl.semaphore_signal(barrier, inc=1, device_id=(h - PLANE, g), device_id_type=MESH)

    kvown[:, :HD] = k_ref[...]
    kvown[:, HD:] = v_ref[...]
    positions = lax.broadcasted_iota(jnp.int32, (BLK, KEEP), 0)
    onehot = (positions == keep_ref[...]).astype(F32).astype(BF16)
    kvbuf[h + 1] = lax.dot_general(
        onehot, kvown[...], (((0,), (0,)), ((), ())), preferred_element_type=F32
    ).astype(BF16)

    @pl.when(h == 0)
    def _():
        kvbuf[0] = kvown[:KEEP, :]

    n_partners = len(partners) + jnp.where(z < NZ - 1, 1, 0) + jnp.where(z > 0, 1, 0)
    pl.semaphore_wait(barrier, n_partners)

    half = BLK // 2

    def w_out(d):
        dst = (y + d) % NY
        return remote(
            w_ref.at[pl.ds(c * half, half), pl.ds(dst * COLS, COLS)],
            wbuf.at[y, pl.ds(c * half, half), :],
            w_send.at[d - 1], w_recv.at[d - 1], (h, at_y(d)),
        )

    def w_in(d):
        src = (y + NY - d) % NY
        ref = wbuf.at[src, pl.ds(c * half, half), :]
        return remote(ref, ref, w_send.at[d - 1], w_recv.at[d - 1], (h, at_y(NY - d)))

    def w_pass(d, core):
        src = (y + NY - d) % NY
        ref = wbuf.at[src, pl.ds(core * half, half), :]
        return remote(ref, ref, wl_send.at[d - 1], wl_recv.at[d - 1], (sib, g))

    w_local = pltpu.make_async_copy(w_ref.at[:, pl.ds(y * COLS, COLS)], wbuf.at[y], w_own)

    def kv_move(slot, device, kind, turn, act):
        ref = kvbuf.at[slot + 1]
        act(remote(ref, ref, kv_send.at[kind, turn], kv_recv.at[slot + 1], (device, g)))

        @pl.when(slot == 0)
        def _():
            anchor = kvbuf.at[0]
            act(remote(anchor, anchor, kv_send.at[kind, NZ], kv_recv.at[0], (device, g)))

    def kv_wait(slot):
        kv_move(slot, sib, 0, 0, lambda copy: copy.wait_recv())

    def column(turn, act):
        slot = (z - turn) * PLANE + 2 * x + c

        @pl.when(z < NZ - 1)
        def _():
            kv_move(slot, h + PLANE, 0, turn, act)

        kv_move(slot, right, 1, turn, act)
        kv_move(slot, left, 2, turn, act)
        kv_move(slot, sib, 3, turn, act)

    def side_slots(turn):
        base = (z - turn) * PLANE + c
        return base + 2 * ((x + NX - 1) % NX), base + 2 * ((x + 1) % NX)

    def sides(turn, act):
        from_left, from_right = side_slots(turn)
        kv_move(jnp.where(c == 0, from_left, from_right), jnp.where(c == 0, right, left), 4, turn, act)
        kv_move(from_left, sib, 5, turn, act)
        kv_move(from_right, sib, 6, turn, act)

    def opposite_slot(turn):
        return (z - turn) * PLANE + c + 2 * ((x + 2) % NX)

    def opposite(turn, act):
        kv_move(opposite_slot(turn), sib, 7, turn, act)

    def event_column(turn):
        @pl.when(turn > 0)
        def _():
            kv_wait((z - turn) * PLANE + 2 * x + c)

        column(turn, start)

    def event_sides(turn):
        for slot in side_slots(turn):
            kv_wait(slot)
        sides(turn, start)

    def event_opposite(turn):
        kv_wait(opposite_slot(turn))
        opposite(turn, start)

    def event_siblings(turn):
        for i in range(NX):
            kv_wait((z - turn) * PLANE + 2 * i + (1 - c))

    event_column(0)
    w_local.start()
    for d in (1, 2, 3):
        w_out(d).start()

    def prepare(j, carry):
        for i in range(QPG):
            rows = q_ref[:, pl.ds(j * 16, 16), i * HD : (i + 1) * HD]
            scaled = rows.reshape(ROWS, HD).astype(F32) * SCALE
            high = scaled.astype(BF16)
            qs[j, i * ROWS : (i + 1) * ROWS, :HD] = high
            qs[j, i * ROWS : (i + 1) * ROWS, HD:] = (scaled - high.astype(F32)).astype(BF16)
        m_s[j] = jnp.full((QROWS, HD), NEG, F32)
        l_s[j] = jnp.zeros((QROWS, HD), F32)
        acc_s[j] = jnp.zeros((QROWS, HD), F32)
        return carry

    lax.fori_loop(0, NCH, prepare, 0)

    def absorb(j, kv, bias):
        keys, vals = kv[:, :HD], kv[:, HD:]
        tiles = [slice(i * HD, (i + 1) * HD) for i in range(kv.shape[0] // HD)]
        scores = lax.dot_general(
            qs[j], jnp.concatenate([keys, keys], axis=1), (((1,), (1,)), ((), ())),
            preferred_element_type=F32,
        )
        scores = scores + bias
        top = functools.reduce(jnp.maximum, [scores[:, t] for t in tiles])
        old = m_s[j]
        new = jnp.maximum(old, jnp.max(top, axis=1, keepdims=True))
        rescale = jnp.exp2(old - new)
        weights = [jnp.exp2(scores[:, t] - new) for t in tiles]
        probs = jnp.concatenate([w.astype(BF16) for w in weights], axis=1)
        l_s[j] = l_s[j] * rescale + functools.reduce(jnp.add, weights)
        acc_s[j] = acc_s[j] * rescale + jnp.dot(probs, vals, preferred_element_type=F32)
        m_s[j] = new

    def column_bias(n, limit):
        return jnp.where(lax.broadcasted_iota(jnp.int32, (1, n), 1) < limit, 0.0, NEG).astype(F32)

    def absorb_plane(j, plane):
        n = PLANE * KEEP
        limit = jnp.where(plane == z, (h % PLANE) * KEEP, n)
        kv = kvbuf[pl.ds(plane * PLANE + 1, PLANE)].reshape(n, 2 * HD)
        absorb(j, kv, column_bias(n, limit))

    def local(j, carry):
        for at, event in ((1, event_sides), (2, event_opposite)):
            pl.when(j == at)(functools.partial(event, 0))
        row = lax.broadcasted_iota(jnp.int32, (QROWS, BLK), 0) % ROWS
        row = (row // 16) * 64 + j * 16 + row % 16
        key = lax.broadcasted_iota(jnp.int32, (QROWS, BLK), 1)
        absorb(j, kvown[...], jnp.where(key <= row, 0.0, NEG).astype(F32))
        return carry

    lax.fori_loop(0, NCH, local, 0)
    event_siblings(0)

    def turn_of(turn, carry):
        def quarter(j, inner):
            for at, event in ((0, event_column), (1, event_sides), (2, event_opposite)):
                pl.when(j == at)(functools.partial(event, turn))
            pl.when(z - turn + 1 >= 2)(lambda: absorb_plane(j, z - turn + 1))
            return inner

        lax.fori_loop(0, NCH, quarter, 0)
        event_siblings(turn)
        return carry

    lax.fori_loop(1, z + 1, turn_of, 0)

    w_local.wait()
    for d in (1, 2, 3):
        w_in(d).wait_recv()
        w_pass(d, c).start()

    def x_move(slot, j, to, kind, recv):
        ref = xbuf.at[slot, j]
        return remote(ref, ref, x_send.at[kind, j], x_recv.at[recv, j], (h, at_y(to)))

    def x_sends(j):
        return [x_move(y, j, 1, 0, 0), x_move(y, j, NY - 1, 1, 1)]

    def x_forward(j):
        slot = jnp.where(c == 0, (y + NY - 1) % NY, (y + 1) % NY)
        return x_move(slot, j, jnp.where(c == 0, 1, NY - 1), 2, 2)

    def x_wait(j, recv, d):
        x_move((y + d) % NY, j, 1, 0, recv).wait_recv()

    def z_move(j):
        return remote(ysend.at[j], zbuf.at[j], z_send.at[j], z_recv.at[j], (h, other))

    def o_move(j, d):
        to = (y + d) % NY
        return remote(
            fbuf.at[j, pl.ds(to * 16, 16), :],
            out_ref.at[pl.ds(j * 16, 16), pl.ds(y * COLS, COLS)],
            o_send.at[d - 1, j], o_recv.at[d - 1, j], (h, at_y(d)),
        )

    def o_wait(j, d):
        src = (y + NY - d) % NY
        ref = out_ref.at[pl.ds(j * 16, 16), pl.ds(src * COLS, COLS)]
        remote(ref, ref, o_send.at[d - 1, j], o_recv.at[d - 1, j], (h, at_y(d))).wait_recv()

    def attend(j):
        def one(i, carry):
            absorb_plane(j, jnp.minimum(z, 1) - i)
            return carry

        lax.fori_loop(0, jnp.minimum(z, 1) + 1, one, 0)
        absorb(j, kvbuf[0], column_bias(KEEP, jnp.where(h > 0, alen_ref[0], 0)))
        total = jnp.sum(l_s[j], axis=1, keepdims=True)
        attended = (acc_s[j] / total).astype(BF16)
        for i in range(QPG):
            xbuf[y, j, :, i * HD : (i + 1) * HD] = attended[i * ROWS : (i + 1) * ROWS]
        for copy in x_sends(j):
            copy.start()

    def relay(j):
        x_wait(j, 0, NY - 1)
        x_wait(j, 1, 1)
        x_forward(j).start()

    def project(j):
        @pl.when(j == 0)
        def _():
            for d in (1, 2, 3):
                w_pass(d, 1 - c).wait_recv()

        x_wait(j, 2, 2)
        ysc[...] = functools.reduce(
            jnp.add,
            [jnp.dot(xbuf[i, j], wbuf[i], preferred_element_type=F32) for i in range(NY)],
        )
        mine = ROWS // 2
        ysend[j] = ysc[pl.ds((1 - zh) * mine, mine), :].astype(BF16)
        z_move(j).start()
        yown[j] = ysc[pl.ds(zh * mine, mine), :]

    def finish(j):
        z_move(j).wait_recv()
        fbuf[j] = (yown[j] + zbuf[j].astype(F32)).astype(BF16)
        for d in (1, 2, 3):
            o_move(j, d).start()
        out_ref[pl.ds(j * 16, 16), pl.ds(y * COLS, COLS)] = fbuf[j, pl.ds(y * 16, 16), :]

    def tail(step, carry):
        for lag, stage in enumerate((attend, relay, project, finish)):
            j = step - lag
            pl.when((j >= 0) & (j < NCH))(functools.partial(stage, j))
        return carry

    lax.fori_loop(0, NCH + 3, tail, 0)

    for d in (1, 2, 3):
        w_out(d).wait_send()
        w_pass(d, c).wait_send()

    def drain(turn, carry):
        column(turn, sent)
        sides(turn, sent)
        opposite(turn, sent)
        return carry

    lax.fori_loop(0, z + 1, drain, 0)

    def drain_tail(j, carry):
        for copy in [*x_sends(j), x_forward(j), z_move(j)]:
            copy.wait_send()
        for d in (1, 2, 3):
            o_move(j, d).wait_send()
            o_wait(j, d)
        return carry

    lax.fori_loop(0, NCH, drain_tail, 0)


def on_device(queries, keys, values, out_weight, keep, anchor_len):
    vmem, dma = pltpu.VMEM, pltpu.SemaphoreType.DMA
    mine = ROWS // 2
    return pl.pallas_call(
        kernel,
        out_shape=jax.ShapeDtypeStruct((BLK // 8, 4 * COLS), BF16),
        in_specs=[pl.BlockSpec(memory_space=pltpu.VMEM)] * 4
        + [pl.BlockSpec(memory_space=pltpu.SMEM), pl.BlockSpec(memory_space=pl.ANY)],
        out_specs=pl.BlockSpec(memory_space=pltpu.VMEM),
        scratch_shapes=[
            vmem((BLK, 2 * HD), BF16),
            vmem((NZ * PLANE + 1, KEEP, 2 * HD), BF16),
            vmem((NCH, QROWS, 2 * HD), BF16),
            vmem((NCH, QROWS, HD), F32),
            vmem((NCH, QROWS, HD), F32),
            vmem((NCH, QROWS, HD), F32),
            vmem((NY, NCH, ROWS, QPG * HD), BF16),
            vmem((NY, BLK, COLS), BF16),
            vmem((ROWS, COLS), F32),
            vmem((NCH, mine, COLS), F32),
            vmem((NCH, mine, COLS), BF16),
            vmem((NCH, mine, COLS), BF16),
            vmem((NCH, mine, COLS), BF16),
            dma((8, NZ + 1)),
            dma((NZ * PLANE + 1,)),
            dma((3,)),
            dma((3,)),
            dma((3,)),
            dma((3,)),
            dma,
            dma((3, NCH)),
            dma((3, NCH)),
            dma((NCH,)),
            dma((NCH,)),
            dma((3, NCH)),
            dma((3, NCH)),
        ],
        compiler_params=pltpu.CompilerParams(
            collective_id=0, has_side_effects=True, vmem_limit_bytes=48 * 2**20
        ),
        cost_estimate=pl.CostEstimate(
            flops=11 * 10**9, bytes_accessed=7 * 10**6, transcendentals=18 * 10**6
        ),
    )(
        queries.reshape(8, BLK // 8, QPG * HD),
        keys,
        values,
        keep.reshape(1, KEEP),
        anchor_len,
        out_weight,
    )


def solution(mesh):
    placed = (
        P("hst", "kv"),
        P("hst", "kv"),
        P("hst", "kv"),
        P("kv", None),
        P("hst", "kv", None),
        P("kv"),
    )
    return jax.shard_map(
        on_device, mesh=mesh, in_specs=placed, out_specs=P(("hst", "kv"), None), check_vma=False
    )
```

```python
import functools
import math

import jax
import jax.numpy as jnp
from jax import lax
from jax.experimental import pallas as pl
from jax.experimental.pallas import tpu as pltpu
from jax.sharding import PartitionSpec as P

HD = 128
QPG = 4
BLK = 512
KEEP = 256
NX, NZ, NY = 4, 4, 4
PLANE = 2 * NX
ANCHOR = NZ * PLANE
NCH = 4
ROWS = BLK // NCH
QROWS = QPG * ROWS
COLS = 1024
SCALE = math.log2(math.e) / math.sqrt(HD)
NEG = -1e30
F32, BF16 = jnp.float32, jnp.bfloat16
MESH = pl.DeviceIdType.MESH


def kernel(
    q_hbm, k_hbm, v_hbm, keep_hbm, alen_hbm, w_ref, out_ref,
    q_ref, keep_ref, alen_ref, in_sem,
    kvown, kvbuf, qs, m_s, l_s, acc_s, xbuf, wbuf, ysc, yown, ysend, zbuf, fbuf,
    kv_send, kv_recv, w_send, w_recv, wl_send, wl_recv, w_own,
    x_send, x_recv, z_send, z_recv, o_send, o_recv,
):
    h = lax.axis_index("hst")
    g = lax.axis_index("kv")
    z, x, c = h // PLANE, (h % PLANE) // 2, h % 2
    zh, y = g // NY, g % NY
    sib = z * PLANE + 2 * x + (1 - c)
    other = (1 - zh) * NY + y

    def at_x(d):
        return z * PLANE + 2 * ((x + d) % NX) + c

    def at_y(d):
        return zh * NY + (y + d) % NY

    def remote(src, dst, send, recv, device):
        return pltpu.make_async_remote_copy(
            src_ref=src, dst_ref=dst, send_sem=send, recv_sem=recv,
            device_id=device, device_id_type=MESH,
        )

    def start(copy):
        copy.start()

    def sent(copy):
        copy.wait_send()

    barrier = pltpu.get_barrier_semaphore()
    partners = [(sib, g), (h, other)]
    for d in (1, 2, 3):
        partners += [(at_x(d), g), (h, at_y(d)), ((h + d * PLANE) % (NZ * PLANE), g)]
    for device in partners:
        pl.semaphore_signal(barrier, inc=1, device_id=device, device_id_type=MESH)

    loads = [
        pltpu.make_async_copy(src, dst, in_sem.at[i])
        for i, (src, dst) in enumerate(
            [
                (k_hbm, kvown.at[:, pl.ds(0, HD)]),
                (v_hbm, kvown.at[:, pl.ds(HD, HD)]),
                (keep_hbm, keep_ref),
                (q_hbm, q_ref),
                (alen_hbm, alen_ref),
            ]
        )
    ]
    for copy in loads:
        copy.start()
    for copy in loads[:3]:
        copy.wait()

    def slot_of(xx, plane, core):
        return xx * 2 * NZ + plane * 2 + core

    positions = lax.broadcasted_iota(jnp.int32, (BLK, KEEP), 0)
    onehot = (positions == keep_ref[...]).astype(F32).astype(BF16)
    kvbuf[slot_of(x, z, c)] = lax.dot_general(
        onehot, kvown[...], (((0,), (0,)), ((), ())), preferred_element_type=F32
    ).astype(BF16)

    @pl.when(h == 0)
    def _():
        kvbuf[ANCHOR] = kvown[:KEEP, :]

    pl.semaphore_wait(barrier, len(partners))

    half = BLK // 2

    def w_out(d):
        dst = (y + d) % NY
        return remote(
            w_ref.at[pl.ds(c * half, half), pl.ds(dst * COLS, COLS)],
            wbuf.at[y, pl.ds(c * half, half), :],
            w_send.at[d - 1], w_recv.at[d - 1], (h, at_y(d)),
        )

    def w_in(d):
        src = (y + NY - d) % NY
        ref = wbuf.at[src, pl.ds(c * half, half), :]
        return remote(ref, ref, w_send.at[d - 1], w_recv.at[d - 1], (h, at_y(NY - d)))

    def w_pass(d, core):
        src = (y + NY - d) % NY
        ref = wbuf.at[src, pl.ds(core * half, half), :]
        return remote(ref, ref, wl_send.at[d - 1], wl_recv.at[d - 1], (sib, g))

    w_local = pltpu.make_async_copy(w_ref.at[:, pl.ds(y * COLS, COLS)], wbuf.at[y], w_own)

    def kv_move(slot, device, kind, turn, act):
        ref = kvbuf.at[slot]
        act(remote(ref, ref, kv_send.at[kind, turn], kv_recv.at[slot], (device, g)))

        @pl.when(slot == 0)
        def _():
            anchor = kvbuf.at[ANCHOR]
            at = NZ + turn if kind == 0 else NZ
            act(remote(anchor, anchor, kv_send.at[kind, at], kv_recv.at[ANCHOR], (device, g)))

    def kv_wait(xx, plane, core):
        kv_move(slot_of(xx, plane, core), sib, 0, 0, lambda copy: copy.wait_recv())

    def upward(act):
        for d in (1, 2, 3):

            @pl.when(z + d < NZ)
            def _():
                kv_move(slot_of(x, z, c), h + d * PLANE, 0, d - 1, act)

    def sideways(plane, act):
        slot = slot_of(x, plane, c)
        kv_move(slot, at_x(1), 1, plane, act)
        kv_move(slot, at_x(3), 2, plane, act)
        kv_move(slot, sib, 3, plane, act)
        kv_move(slot, at_x(2), 4, plane, act)

    def across(d, plane, act):
        kv_move(slot_of((x + d) % NX, plane, c), sib, 4 + d, plane, act)

    def each_plane(body):
        lax.fori_loop(0, z + 1, lambda plane, carry: (body(plane), carry)[1], 0)

    def event_column(turn):
        kv_wait(x, z - turn, c)
        sideways(z - turn, start)

    def event_side(d):
        def one(plane):
            kv_wait((x + d) % NX, plane, c)
            across(d, plane, start)

        each_plane(one)

    def event_sibling(d):
        each_plane(lambda plane: kv_wait((x + d) % NX, plane, 1 - c))

    upward(start)
    sideways(z, start)
    w_local.start()
    for d in (1, 2, 3):
        w_out(d).start()

    @pl.when(z % 2 == 0)
    def _():
        def clear(xx, carry):
            kvbuf[pl.ds(slot_of(xx, z + 1, 0), 2)] = jnp.zeros((2, KEEP, 2 * HD), BF16)
            return carry

        lax.fori_loop(0, NX, clear, 0)

    for copy in loads[3:]:
        copy.wait()

    def prepare(j, carry):
        for i in range(QPG):
            rows = q_ref[:, pl.ds(j * 16, 16), i * HD : (i + 1) * HD]
            scaled = rows.reshape(ROWS, HD).astype(F32) * SCALE
            high = scaled.astype(BF16)
            qs[j, i * ROWS : (i + 1) * ROWS, :HD] = high
            qs[j, i * ROWS : (i + 1) * ROWS, HD:] = (scaled - high.astype(F32)).astype(BF16)
        m_s[j] = jnp.full((QROWS, HD), NEG, F32)
        l_s[j] = jnp.zeros((QROWS, HD), F32)
        acc_s[j] = jnp.zeros((QROWS, HD), F32)
        return carry

    lax.fori_loop(0, NCH, prepare, 0)

    def absorb(j, kv, bias):
        keys, vals = kv[:, :HD], kv[:, HD:]
        tiles = [slice(i * HD, (i + 1) * HD) for i in range(kv.shape[0] // HD)]
        scores = lax.dot_general(
            qs[j], jnp.concatenate([keys, keys], axis=1), (((1,), (1,)), ((), ())),
            preferred_element_type=F32,
        )
        scores = scores + bias
        top = functools.reduce(jnp.maximum, [scores[:, t] for t in tiles])
        old = m_s[j]
        new = jnp.maximum(old, jnp.max(top, axis=1, keepdims=True))
        rescale = jnp.exp2(old - new)
        weights = [jnp.exp2(scores[:, t] - new) for t in tiles]
        probs = jnp.concatenate([w.astype(BF16) for w in weights], axis=1)
        l_s[j] = l_s[j] * rescale + functools.reduce(jnp.add, weights)
        acc_s[j] = acc_s[j] * rescale + jnp.dot(probs, vals, preferred_element_type=F32)
        m_s[j] = new

    def column_bias(n, limit):
        return jnp.where(lax.broadcasted_iota(jnp.int32, (1, n), 1) < limit, 0.0, NEG).astype(F32)

    def absorb_column(j, xx, first, planes):
        n = planes * 2 * KEEP
        own = jnp.where(xx < x, 2 * KEEP, jnp.where(xx == x, c * KEEP, 0))
        limit = z * 2 * KEEP + own - first * 2 * KEEP
        kv = kvbuf[pl.ds(slot_of(xx, first, 0), 2 * planes)].reshape(n, 2 * HD)
        absorb(j, kv, column_bias(n, limit))

    def each_chunk(body):
        lax.fori_loop(0, NCH, lambda j, carry: (body(j), carry)[1], 0, unroll=2)

    def local(j):
        row = lax.broadcasted_iota(jnp.int32, (QROWS, BLK), 0) % ROWS
        row = (row // 16) * 64 + j * 16 + row % 16
        key = lax.broadcasted_iota(jnp.int32, (QROWS, BLK), 1)
        absorb(j, kvown[...], jnp.where(key <= row, 0.0, NEG).astype(F32))

    each_chunk(local)

    pl.when(z >= 1)(functools.partial(event_column, 1))
    kv_wait(x, z, 1 - c)
    pl.when(z >= 1)(lambda: kv_wait(x, z - 1, 1 - c))
    each_chunk(lambda j: absorb_column(j, x, (z // 2) * 2, 2))
    for turn in (2, 3):
        pl.when(z >= turn)(functools.partial(event_column, turn))
    for turn in (2, 3):
        pl.when(z >= turn)(lambda: kv_wait(x, z - turn, 1 - c))
    pl.when(z >= 2)(lambda: each_chunk(lambda j: absorb_column(j, x, 0, 2)))

    event_side(3)
    event_side(1)

    def x_move(j, d):
        ref = xbuf.at[y, j]
        return remote(ref, ref, x_send.at[d - 1, j], x_recv.at[d - 1, j], (h, at_y(d)))

    def x_wait(j, d):
        ref = xbuf.at[(y + NY - d) % NY, j]
        remote(ref, ref, x_send.at[d - 1, j], x_recv.at[d - 1, j], (h, at_y(d))).wait_recv()

    def z_move(j):
        return remote(ysend.at[j], zbuf.at[j], z_send.at[j], z_recv.at[j], (h, other))

    def o_move(j, d):
        to = (y + d) % NY
        return remote(
            fbuf.at[j, pl.ds(to * 16, 16), :],
            out_ref.at[pl.ds(j * 16, 16), pl.ds(y * COLS, COLS)],
            o_send.at[d - 1, j], o_recv.at[d - 1, j], (h, at_y(d)),
        )

    def o_wait(j, d):
        src = (y + NY - d) % NY
        ref = out_ref.at[pl.ds(j * 16, 16), pl.ds(src * COLS, COLS)]
        remote(ref, ref, o_send.at[d - 1, j], o_recv.at[d - 1, j], (h, at_y(d))).wait_recv()

    def attend(j):
        def one(i, carry):
            d = jnp.where(i == 0, 3, i)

            @pl.when(j == 0)
            def _():
                pl.when(i == 2)(lambda: event_side(2))
                event_sibling(d)

            xx = (x + d) % NX
            pl.when(z >= 2)(lambda: absorb_column(j, xx, 0, 4))
            pl.when(z < 2)(lambda: absorb_column(j, xx, 0, 2))
            return carry

        lax.fori_loop(0, 3, one, 0)
        absorb(j, kvbuf[ANCHOR], column_bias(KEEP, jnp.where(h > 0, alen_ref[0], 0)))
        total = jnp.sum(l_s[j], axis=1, keepdims=True)
        attended = (acc_s[j] / total).astype(BF16)
        for i in range(QPG):
            xbuf[y, j, :, i * HD : (i + 1) * HD] = attended[i * ROWS : (i + 1) * ROWS]
        for d in (1, 3, 2):
            x_move(j, d).start()

        @pl.when(j == 1)
        def _():
            w_local.wait()
            for d in (1, 2, 3):
                w_in(d).wait_recv()
                w_pass(d, c).start()

    def project(j):
        @pl.when(j == 0)
        def _():
            for d in (1, 2, 3):
                w_pass(d, 1 - c).wait_recv()

        for d in (1, 2, 3):
            x_wait(j, d)
        ysc[...] = functools.reduce(
            jnp.add,
            [jnp.dot(xbuf[i, j], wbuf[i], preferred_element_type=F32) for i in range(NY)],
        )
        mine = ROWS // 2
        ysend[j] = ysc[pl.ds((1 - zh) * mine, mine), :].astype(BF16)
        z_move(j).start()
        yown[j] = ysc[pl.ds(zh * mine, mine), :]

    def finish(j):
        z_move(j).wait_recv()
        fbuf[j] = (yown[j] + zbuf[j].astype(F32)).astype(BF16)
        for d in (1, 2, 3):
            o_move(j, d).start()
        out_ref[pl.ds(j * 16, 16), pl.ds(y * COLS, COLS)] = fbuf[j, pl.ds(y * 16, 16), :]

    def tail(step, carry):
        for lag, stage in ((0, attend), (2, project), (3, finish)):
            j = step - lag
            pl.when((j >= 0) & (j < NCH))(functools.partial(stage, j))
        return carry

    lax.fori_loop(0, NCH + 3, tail, 0)

    for d in (1, 2, 3):
        w_out(d).wait_send()
        w_pass(d, c).wait_send()

    upward(sent)

    def drain(plane):
        sideways(plane, sent)
        for d in (1, 2, 3):
            across(d, plane, sent)

    each_plane(drain)

    def drain_tail(j, carry):
        z_move(j).wait_send()
        for d in (1, 2, 3):
            x_move(j, d).wait_send()
            o_move(j, d).wait_send()
            o_wait(j, d)
        return carry

    lax.fori_loop(0, NCH, drain_tail, 0)


def on_device(queries, keys, values, out_weight, keep, anchor_len):
    vmem, dma = pltpu.VMEM, pltpu.SemaphoreType.DMA
    mine = ROWS // 2
    return pl.pallas_call(
        kernel,
        out_shape=jax.ShapeDtypeStruct((BLK // 8, 4 * COLS), BF16),
        in_specs=[pl.BlockSpec(memory_space=pl.ANY)] * 6,
        out_specs=pl.BlockSpec(memory_space=pltpu.VMEM),
        scratch_shapes=[
            vmem((8, BLK // 8, QPG * HD), BF16),
            vmem((1, KEEP), jnp.int32),
            pltpu.SMEM((1,), jnp.int32),
            dma((5,)),
            vmem((BLK, 2 * HD), BF16),
            vmem((NZ * PLANE + 1, KEEP, 2 * HD), BF16),
            vmem((NCH, QROWS, 2 * HD), BF16),
            vmem((NCH, QROWS, HD), F32),
            vmem((NCH, QROWS, HD), F32),
            vmem((NCH, QROWS, HD), F32),
            vmem((NY, NCH, ROWS, QPG * HD), BF16),
            vmem((NY, BLK, COLS), BF16),
            vmem((ROWS, COLS), F32),
            vmem((NCH, mine, COLS), F32),
            vmem((NCH, mine, COLS), BF16),
            vmem((NCH, mine, COLS), BF16),
            vmem((NCH, mine, COLS), BF16),
            dma((8, NZ + 3)),
            dma((NZ * PLANE + 1,)),
            dma((3,)),
            dma((3,)),
            dma((3,)),
            dma((3,)),
            dma,
            dma((3, NCH)),
            dma((3, NCH)),
            dma((NCH,)),
            dma((NCH,)),
            dma((3, NCH)),
            dma((3, NCH)),
        ],
        compiler_params=pltpu.CompilerParams(
            collective_id=0, has_side_effects=True, vmem_limit_bytes=48 * 2**20
        ),
        cost_estimate=pl.CostEstimate(
            flops=11 * 10**9, bytes_accessed=7 * 10**6, transcendentals=18 * 10**6
        ),
    )(
        queries.reshape(8, BLK // 8, QPG * HD),
        keys,
        values,
        keep.reshape(1, KEEP),
        anchor_len,
        out_weight,
    )


def solution(mesh):
    placed = (
        P("hst", "kv"),
        P("hst", "kv"),
        P("hst", "kv"),
        P("kv", None),
        P("hst", "kv", None),
        P("kv"),
    )
    return jax.shard_map(
        on_device, mesh=mesh, in_specs=placed, out_specs=P(("hst", "kv"), None), check_vma=False
    )
```

```python
import functools
import math

import jax
import jax.numpy as jnp
from jax import lax
from jax.experimental import pallas as pl
from jax.experimental.pallas import tpu as pltpu
from jax.sharding import PartitionSpec as P

HD = 128
QPG = 4
BLK = 512
KEEP = 256
NX, NZ, NY = 4, 4, 4
PLANE = 2 * NX
ANCHOR = NZ * PLANE
NCH = 4
ROWS = BLK // NCH
QROWS = QPG * ROWS
COLS = 1024
SCALE = math.log2(math.e) / math.sqrt(HD)
NEG = -1e30
F32, BF16 = jnp.float32, jnp.bfloat16
MESH = pl.DeviceIdType.MESH


def kernel(
    q_hbm, k_hbm, v_hbm, keep_hbm, alen_hbm, w_ref, out_ref,
    q_ref, keep_ref, alen_ref, in_sem,
    kvown, kvbuf, qs, m_s, l_s, acc_s, xbuf, wbuf, ysc, yown, ysend, zbuf, fbuf,
    kv_send, kv_recv, w_send, w_recv, wl_send, wl_recv, w_own,
    x_send, x_recv, z_send, z_recv, o_send, o_recv,
):
    h = lax.axis_index("hst")
    g = lax.axis_index("kv")
    z, x, c = h // PLANE, (h % PLANE) // 2, h % 2
    zh, y = g // NY, g % NY
    sib = z * PLANE + 2 * x + (1 - c)
    other = (1 - zh) * NY + y

    def at_x(d):
        return z * PLANE + 2 * ((x + d) % NX) + c

    def at_y(d):
        return zh * NY + (y + d) % NY

    def remote(src, dst, send, recv, device):
        return pltpu.make_async_remote_copy(
            src_ref=src, dst_ref=dst, send_sem=send, recv_sem=recv,
            device_id=device, device_id_type=MESH,
        )

    def start(copy):
        copy.start()

    def sent(copy):
        copy.wait_send()

    barrier = pltpu.get_barrier_semaphore()
    partners = [(sib, g), (h, other)]
    for d in (1, 2, 3):
        partners += [(at_x(d), g), (h, at_y(d)), ((h + d * PLANE) % (NZ * PLANE), g)]
    for device in partners:
        pl.semaphore_signal(barrier, inc=1, device_id=device, device_id_type=MESH)

    loads = [
        pltpu.make_async_copy(src, dst, in_sem.at[i])
        for i, (src, dst) in enumerate(
            [
                (k_hbm, kvown.at[:, pl.ds(0, HD)]),
                (v_hbm, kvown.at[:, pl.ds(HD, HD)]),
                (keep_hbm, keep_ref),
                (q_hbm, q_ref),
                (alen_hbm, alen_ref),
            ]
        )
    ]
    for copy in loads:
        copy.start()
    for copy in loads[:3]:
        copy.wait()

    def slot_of(xx, plane, core):
        return xx * 2 * NZ + plane * 2 + core

    positions = lax.broadcasted_iota(jnp.int32, (BLK, KEEP), 0)
    onehot = (positions == keep_ref[...]).astype(F32).astype(BF16)
    kvbuf[slot_of(x, z, c)] = lax.dot_general(
        onehot, kvown[...], (((0,), (0,)), ((), ())), preferred_element_type=F32
    ).astype(BF16)

    @pl.when(h == 0)
    def _():
        kvbuf[ANCHOR] = kvown[:KEEP, :]

    pl.semaphore_wait(barrier, len(partners))

    half = BLK // 2

    def w_out(d):
        dst = (y + d) % NY
        return remote(
            w_ref.at[pl.ds(c * half, half), pl.ds(dst * COLS, COLS)],
            wbuf.at[y, pl.ds(c * half, half), :],
            w_send.at[d - 1], w_recv.at[d - 1], (h, at_y(d)),
        )

    def w_in(d):
        src = (y + NY - d) % NY
        ref = wbuf.at[src, pl.ds(c * half, half), :]
        return remote(ref, ref, w_send.at[d - 1], w_recv.at[d - 1], (h, at_y(NY - d)))

    def w_pass(d, core):
        src = (y + NY - d) % NY
        ref = wbuf.at[src, pl.ds(core * half, half), :]
        return remote(ref, ref, wl_send.at[d - 1], wl_recv.at[d - 1], (sib, g))

    w_local = pltpu.make_async_copy(w_ref.at[:, pl.ds(y * COLS, COLS)], wbuf.at[y], w_own)

    def kv_move(slot, device, kind, turn, act):
        ref = kvbuf.at[slot]
        act(remote(ref, ref, kv_send.at[kind, turn], kv_recv.at[slot], (device, g)))

        @pl.when(slot == 0)
        def _():
            anchor = kvbuf.at[ANCHOR]
            at = NZ + turn if kind == 0 else NZ
            act(remote(anchor, anchor, kv_send.at[kind, at], kv_recv.at[ANCHOR], (device, g)))

    def kv_wait(xx, plane, core):
        kv_move(slot_of(xx, plane, core), sib, 0, 0, lambda copy: copy.wait_recv())

    def upward(act):
        for d in (1, 2, 3):

            @pl.when(z + d < NZ)
            def _():
                kv_move(slot_of(x, z, c), h + d * PLANE, 0, d - 1, act)

    def sideways(turn, act):
        plane = z - turn
        slot = slot_of(x, plane, c)
        kv_move(slot, at_x(1), 1, plane, act)
        kv_move(slot, at_x(3), 2, plane, act)
        kv_move(slot, sib, 3, plane, act)
        kv_move(slot, at_x(2), 4, plane, act)

    def across(d, turn, act):
        plane = z - turn
        kv_move(slot_of((x + d) % NX, plane, c), sib, 4 + d, plane, act)

    def event_column(turn):
        kv_wait(x, z - turn, c)
        sideways(turn, start)

    def event_sides(turn):
        for d in (3, 1):
            kv_wait((x + d) % NX, z - turn, c)
            across(d, turn, start)

    def event_opposite(turn):
        kv_wait((x + 2) % NX, z - turn, c)
        across(2, turn, start)

    def event_sibling(d, turn):
        kv_wait((x + d) % NX, z - turn, 1 - c)

    def event(what, turn, *args):
        pl.when(z >= turn)(lambda: what(*args, turn))

    upward(start)
    sideways(0, start)
    w_local.start()
    for d in (1, 2, 3):
        w_out(d).start()

    @pl.when(z % 2 == 0)
    def _():
        def clear(xx, carry):
            kvbuf[pl.ds(slot_of(xx, z + 1, 0), 2)] = jnp.zeros((2, KEEP, 2 * HD), BF16)
            return carry

        lax.fori_loop(0, NX, clear, 0)

    for copy in loads[3:]:
        copy.wait()

    def prepare(j, carry):
        for i in range(QPG):
            rows = q_ref[:, pl.ds(j * 16, 16), i * HD : (i + 1) * HD]
            scaled = rows.reshape(ROWS, HD).astype(F32) * SCALE
            high = scaled.astype(BF16)
            qs[j, i * ROWS : (i + 1) * ROWS, :HD] = high
            qs[j, i * ROWS : (i + 1) * ROWS, HD:] = (scaled - high.astype(F32)).astype(BF16)
        m_s[j] = jnp.full((QROWS, HD), NEG, F32)
        l_s[j] = jnp.zeros((QROWS, HD), F32)
        acc_s[j] = jnp.zeros((QROWS, HD), F32)
        return carry

    lax.fori_loop(0, NCH, prepare, 0)

    def absorb(j, kv, bias):
        keys, vals = kv[:, :HD], kv[:, HD:]
        tiles = [slice(i * HD, (i + 1) * HD) for i in range(kv.shape[0] // HD)]
        scores = lax.dot_general(
            qs[j], jnp.concatenate([keys, keys], axis=1), (((1,), (1,)), ((), ())),
            preferred_element_type=F32,
        )
        scores = scores + bias
        top = functools.reduce(jnp.maximum, [scores[:, t] for t in tiles])
        old = m_s[j]
        new = jnp.maximum(old, jnp.max(top, axis=1, keepdims=True))
        rescale = jnp.exp2(old - new)
        weights = [jnp.exp2(scores[:, t] - new) for t in tiles]
        probs = jnp.concatenate([w.astype(BF16) for w in weights], axis=1)
        l_s[j] = l_s[j] * rescale + functools.reduce(jnp.add, weights)
        acc_s[j] = acc_s[j] * rescale + jnp.dot(probs, vals, preferred_element_type=F32)
        m_s[j] = new

    def column_bias(n, limit):
        return jnp.where(lax.broadcasted_iota(jnp.int32, (1, n), 1) < limit, 0.0, NEG).astype(F32)

    def absorb_column(j, xx, first, planes):
        n = planes * 2 * KEEP
        own = jnp.where(xx < x, 2 * KEEP, jnp.where(xx == x, c * KEEP, 0))
        limit = z * 2 * KEEP + own - first * 2 * KEEP
        kv = kvbuf[pl.ds(slot_of(xx, first, 0), 2 * planes)].reshape(n, 2 * HD)
        absorb(j, kv, column_bias(n, limit))

    def each_chunk(body):
        lax.fori_loop(0, NCH, lambda j, carry: (body(j), carry)[1], 0, unroll=2)

    def local(j):
        row = lax.broadcasted_iota(jnp.int32, (QROWS, BLK), 0) % ROWS
        row = (row // 16) * 64 + j * 16 + row % 16
        key = lax.broadcasted_iota(jnp.int32, (QROWS, BLK), 1)
        absorb(j, kvown[...], jnp.where(key <= row, 0.0, NEG).astype(F32))

    each_chunk(local)

    def half_column(d):
        event(event_sibling, 0, d)
        event(event_sibling, 1, d)
        each_chunk(lambda j: absorb_column(j, (x + d) % NX, z // 2 * 2, 2))

    event(event_column, 1)
    half_column(0)
    event(event_column, 2)
    event(event_column, 3)
    event(event_sides, 0)
    event(event_sides, 1)
    pl.when(z >= 2)(lambda: half_column(3))
    event(event_opposite, 0)
    event(event_opposite, 1)
    pl.when(z >= 2)(lambda: half_column(1))
    pl.when(z >= 2)(lambda: half_column(2))
    event(event_sides, 2)
    event(event_opposite, 2)
    event(event_sides, 3)

    def x_move(j, d):
        ref = xbuf.at[y, j]
        return remote(ref, ref, x_send.at[d - 1, j], x_recv.at[d - 1, j], (h, at_y(d)))

    def x_wait(j, d):
        ref = xbuf.at[(y + NY - d) % NY, j]
        remote(ref, ref, x_send.at[d - 1, j], x_recv.at[d - 1, j], (h, at_y(d))).wait_recv()

    def z_move(j):
        return remote(ysend.at[j], zbuf.at[j], z_send.at[j], z_recv.at[j], (h, other))

    def o_move(j, d):
        to = (y + d) % NY
        return remote(
            fbuf.at[j, pl.ds(to * 16, 16), :],
            out_ref.at[pl.ds(j * 16, 16), pl.ds(y * COLS, COLS)],
            o_send.at[d - 1, j], o_recv.at[d - 1, j], (h, at_y(d)),
        )

    def o_wait(j, d):
        src = (y + NY - d) % NY
        ref = out_ref.at[pl.ds(j * 16, 16), pl.ds(src * COLS, COLS)]
        remote(ref, ref, o_send.at[d - 1, j], o_recv.at[d - 1, j], (h, at_y(d))).wait_recv()

    def attend(j):
        def one(i, carry):
            d = jnp.where(i == 0, 0, jnp.where(i == 1, 3, jnp.where(i == 2, 1, 2)))

            @pl.when(j == 0)
            def _():
                pl.when((i == 3) & (z >= 3))(lambda: event_opposite(3))
                turn = jnp.where(z >= 2, 2, 0)
                event(event_sibling, turn, d)
                event(event_sibling, turn + 1, d)

            absorb_column(j, (x + d) % NX, 0, 2)
            return carry

        lax.fori_loop(jnp.where(z >= 2, 0, 1), 4, one, 0)
        absorb(j, kvbuf[ANCHOR], column_bias(KEEP, jnp.where(h > 0, alen_ref[0], 0)))
        total = jnp.sum(l_s[j], axis=1, keepdims=True)
        attended = (acc_s[j] / total).astype(BF16)
        for i in range(QPG):
            xbuf[y, j, :, i * HD : (i + 1) * HD] = attended[i * ROWS : (i + 1) * ROWS]
        for d in (1, 3, 2):
            x_move(j, d).start()

        @pl.when(j == 1)
        def _():
            w_local.wait()
            for d in (1, 2, 3):
                w_in(d).wait_recv()
                w_pass(d, c).start()

    def project(j):
        @pl.when(j == 0)
        def _():
            for d in (1, 2, 3):
                w_pass(d, 1 - c).wait_recv()

        for d in (1, 2, 3):
            x_wait(j, d)
        ysc[...] = functools.reduce(
            jnp.add,
            [jnp.dot(xbuf[i, j], wbuf[i], preferred_element_type=F32) for i in range(NY)],
        )
        mine = ROWS // 2
        ysend[j] = ysc[pl.ds((1 - zh) * mine, mine), :].astype(BF16)
        z_move(j).start()
        yown[j] = ysc[pl.ds(zh * mine, mine), :]

    def finish(j):
        z_move(j).wait_recv()
        fbuf[j] = (yown[j] + zbuf[j].astype(F32)).astype(BF16)
        for d in (1, 2, 3):
            o_move(j, d).start()
        out_ref[pl.ds(j * 16, 16), pl.ds(y * COLS, COLS)] = fbuf[j, pl.ds(y * 16, 16), :]

    def tail(step, carry):
        for lag, stage in ((0, attend), (2, project), (3, finish)):
            j = step - lag
            pl.when((j >= 0) & (j < NCH))(functools.partial(stage, j))
        return carry

    lax.fori_loop(0, NCH + 3, tail, 0)

    for d in (1, 2, 3):
        w_out(d).wait_send()
        w_pass(d, c).wait_send()

    upward(sent)

    def drain(turn, carry):
        sideways(turn, sent)
        for d in (1, 2, 3):
            across(d, turn, sent)
        return carry

    lax.fori_loop(0, z + 1, drain, 0)

    def drain_tail(j, carry):
        z_move(j).wait_send()
        for d in (1, 2, 3):
            x_move(j, d).wait_send()
            o_move(j, d).wait_send()
            o_wait(j, d)
        return carry

    lax.fori_loop(0, NCH, drain_tail, 0)


def on_device(queries, keys, values, out_weight, keep, anchor_len):
    vmem, dma = pltpu.VMEM, pltpu.SemaphoreType.DMA
    mine = ROWS // 2
    return pl.pallas_call(
        kernel,
        out_shape=jax.ShapeDtypeStruct((BLK // 8, 4 * COLS), BF16),
        in_specs=[pl.BlockSpec(memory_space=pl.ANY)] * 6,
        out_specs=pl.BlockSpec(memory_space=pltpu.VMEM),
        scratch_shapes=[
            vmem((8, BLK // 8, QPG * HD), BF16),
            vmem((1, KEEP), jnp.int32),
            pltpu.SMEM((1,), jnp.int32),
            dma((5,)),
            vmem((BLK, 2 * HD), BF16),
            vmem((NZ * PLANE + 1, KEEP, 2 * HD), BF16),
            vmem((NCH, QROWS, 2 * HD), BF16),
            vmem((NCH, QROWS, HD), F32),
            vmem((NCH, QROWS, HD), F32),
            vmem((NCH, QROWS, HD), F32),
            vmem((NY, NCH, ROWS, QPG * HD), BF16),
            vmem((NY, BLK, COLS), BF16),
            vmem((ROWS, COLS), F32),
            vmem((NCH, mine, COLS), F32),
            vmem((NCH, mine, COLS), BF16),
            vmem((NCH, mine, COLS), BF16),
            vmem((NCH, mine, COLS), BF16),
            dma((8, NZ + 3)),
            dma((NZ * PLANE + 1,)),
            dma((3,)),
            dma((3,)),
            dma((3,)),
            dma((3,)),
            dma,
            dma((3, NCH)),
            dma((3, NCH)),
            dma((NCH,)),
            dma((NCH,)),
            dma((3, NCH)),
            dma((3, NCH)),
        ],
        compiler_params=pltpu.CompilerParams(
            collective_id=0, has_side_effects=True, vmem_limit_bytes=60 * 2**20
        ),
        cost_estimate=pl.CostEstimate(
            flops=11 * 10**9, bytes_accessed=7 * 10**6, transcendentals=18 * 10**6
        ),
    )(
        queries.reshape(8, BLK // 8, QPG * HD),
        keys,
        values,
        keep.reshape(1, KEEP),
        anchor_len,
        out_weight,
    )


def solution(mesh):
    placed = (
        P("hst", "kv"),
        P("hst", "kv"),
        P("hst", "kv"),
        P("kv", None),
        P("hst", "kv", None),
        P("kv"),
    )
    return jax.shard_map(
        on_device, mesh=mesh, in_specs=placed, out_specs=P(("hst", "kv"), None), check_vma=False
    )
```

```python
import functools
import math

import jax
import jax.numpy as jnp
from jax import lax
from jax.experimental import pallas as pl
from jax.experimental.pallas import tpu as pltpu
from jax.sharding import PartitionSpec as P

HD = 128
QPG = 4
BLK = 512
KEEP = 256
NX, NZ, NY = 4, 4, 4
PLANE = 2 * NX
ANCHOR = NZ * PLANE
NCH = 4
ROWS = BLK // NCH
QROWS = QPG * ROWS
COLS = 1024
SCALE = math.log2(math.e) / math.sqrt(HD)
NEG = -1e30
F32, BF16 = jnp.float32, jnp.bfloat16
MESH = pl.DeviceIdType.MESH


def kernel(
    q_hbm, k_hbm, v_hbm, keep_hbm, alen_hbm, w_ref, out_ref,
    q_ref, keep_ref, alen_ref, in_sem,
    kvown, kvbuf, qs, m_s, l_s, acc_s, xbuf, wbuf, ysc, yown, ysend, zbuf, fbuf,
    kv_send, kv_recv, w_send, w_recv, wl_send, wl_recv, w_own,
    x_send, x_recv, z_send, z_recv, o_send, o_recv,
):
    h = lax.axis_index("hst")
    g = lax.axis_index("kv")
    z, x, c = h // PLANE, (h % PLANE) // 2, h % 2
    zh, y = g // NY, g % NY
    sib = z * PLANE + 2 * x + (1 - c)
    other = (1 - zh) * NY + y

    def at_x(d):
        return z * PLANE + 2 * ((x + d) % NX) + c

    def at_y(d):
        return zh * NY + (y + d) % NY

    def remote(src, dst, send, recv, device):
        return pltpu.make_async_remote_copy(
            src_ref=src, dst_ref=dst, send_sem=send, recv_sem=recv,
            device_id=device, device_id_type=MESH,
        )

    def start(copy):
        copy.start()

    def sent(copy):
        copy.wait_send()

    barrier = pltpu.get_barrier_semaphore()
    partners = [(sib, g), (h, other)]
    for d in (1, 2, 3):
        partners += [(at_x(d), g), (h, at_y(d)), ((h + d * PLANE) % (NZ * PLANE), g)]
    for device in partners:
        pl.semaphore_signal(barrier, inc=1, device_id=device, device_id_type=MESH)

    loads = [
        pltpu.make_async_copy(src, dst, in_sem.at[i])
        for i, (src, dst) in enumerate(
            [
                (k_hbm, kvown.at[:, pl.ds(0, HD)]),
                (v_hbm, kvown.at[:, pl.ds(HD, HD)]),
                (keep_hbm, keep_ref),
                (q_hbm, q_ref),
                (alen_hbm, alen_ref),
            ]
        )
    ]
    for copy in loads:
        copy.start()
    for copy in loads[:3]:
        copy.wait()

    def slot_of(xx, plane, core):
        return xx * 2 * NZ + plane * 2 + core

    positions = lax.broadcasted_iota(jnp.int32, (BLK, KEEP), 0)
    onehot = (positions == keep_ref[...]).astype(F32).astype(BF16)
    kvbuf[slot_of(x, z, c)] = lax.dot_general(
        onehot, kvown[...], (((0,), (0,)), ((), ())), preferred_element_type=F32
    ).astype(BF16)

    @pl.when(h == 0)
    def _():
        kvbuf[ANCHOR] = kvown[:KEEP, :]

    pl.semaphore_wait(barrier, len(partners))

    half = BLK // 2

    def w_out(d):
        dst = (y + d) % NY
        return remote(
            w_ref.at[pl.ds(c * half, half), pl.ds(dst * COLS, COLS)],
            wbuf.at[y, pl.ds(c * half, half), :],
            w_send.at[d - 1], w_recv.at[d - 1], (h, at_y(d)),
        )

    def w_in(d):
        src = (y + NY - d) % NY
        ref = wbuf.at[src, pl.ds(c * half, half), :]
        return remote(ref, ref, w_send.at[d - 1], w_recv.at[d - 1], (h, at_y(NY - d)))

    def w_pass(d, core):
        src = (y + NY - d) % NY
        ref = wbuf.at[src, pl.ds(core * half, half), :]
        return remote(ref, ref, wl_send.at[d - 1], wl_recv.at[d - 1], (sib, g))

    w_local = pltpu.make_async_copy(w_ref.at[:, pl.ds(y * COLS, COLS)], wbuf.at[y], w_own)

    def kv_move(slot, device, kind, turn, act):
        ref = kvbuf.at[slot]
        act(remote(ref, ref, kv_send.at[kind, turn], kv_recv.at[slot], (device, g)))

        @pl.when(slot == 0)
        def _():
            anchor = kvbuf.at[ANCHOR]
            at = NZ + turn if kind == 0 else NZ
            act(remote(anchor, anchor, kv_send.at[kind, at], kv_recv.at[ANCHOR], (device, g)))

    def kv_wait(xx, plane, core):
        kv_move(slot_of(xx, plane, core), sib, 0, 0, lambda copy: copy.wait_recv())

    def upward(act):
        for d in (1, 2, 3):

            @pl.when(z + d < NZ)
            def _():
                kv_move(slot_of(x, z, c), h + d * PLANE, 0, d - 1, act)

    def sideways(turn, act):
        plane = z - turn
        slot = slot_of(x, plane, c)
        kv_move(slot, at_x(1), 1, plane, act)
        kv_move(slot, at_x(3), 2, plane, act)
        kv_move(slot, sib, 3, plane, act)
        kv_move(slot, at_x(2), 4, plane, act)

    def across(d, turn, act):
        plane = z - turn
        kv_move(slot_of((x + d) % NX, plane, c), sib, 4 + d, plane, act)

    def event_column(turn):
        kv_wait(x, z - turn, c)
        sideways(turn, start)

    def event_sides(turn):
        for d in (3, 1):
            kv_wait((x + d) % NX, z - turn, c)
            across(d, turn, start)

    def event_opposite(turn):
        kv_wait((x + 2) % NX, z - turn, c)
        across(2, turn, start)

    def event_sibling(d, turn):
        kv_wait((x + d) % NX, z - turn, 1 - c)

    def event(what, turn, *args):
        pl.when(z >= turn)(lambda: what(*args, turn))

    upward(start)
    sideways(0, start)
    w_local.start()
    for d in (1, 2, 3):
        w_out(d).start()

    @pl.when(z % 2 == 0)
    def _():
        def clear(xx, carry):
            kvbuf[pl.ds(slot_of(xx, z + 1, 0), 2)] = jnp.zeros((2, KEEP, 2 * HD), BF16)
            return carry

        lax.fori_loop(0, NX, clear, 0)

    for copy in loads[3:]:
        copy.wait()

    def prepare(j, carry):
        for i in range(QPG):
            rows = q_ref[:, pl.ds(j * 16, 16), i * HD : (i + 1) * HD]
            scaled = rows.reshape(ROWS, HD).astype(F32) * SCALE
            high = scaled.astype(BF16)
            qs[j, i * ROWS : (i + 1) * ROWS, :HD] = high
            qs[j, i * ROWS : (i + 1) * ROWS, HD:] = (scaled - high.astype(F32)).astype(BF16)
        m_s[j] = jnp.full((QROWS, HD), NEG, F32)
        l_s[j] = jnp.zeros((QROWS, HD), F32)
        acc_s[j] = jnp.zeros((QROWS, HD), F32)
        return carry

    lax.fori_loop(0, NCH, prepare, 0)

    def absorb(j, kv, bias):
        keys, vals = kv[:, :HD], kv[:, HD:]
        tiles = [slice(i * HD, (i + 1) * HD) for i in range(kv.shape[0] // HD)]
        scores = lax.dot_general(
            qs[j], jnp.concatenate([keys, keys], axis=1), (((1,), (1,)), ((), ())),
            preferred_element_type=F32,
        )
        scores = scores + bias
        top = functools.reduce(jnp.maximum, [scores[:, t] for t in tiles])
        old = m_s[j]
        new = jnp.maximum(old, jnp.max(top, axis=1, keepdims=True))
        rescale = jnp.exp2(old - new)
        weights = [jnp.exp2(scores[:, t] - new) for t in tiles]
        probs = jnp.concatenate([w.astype(BF16) for w in weights], axis=1)
        l_s[j] = l_s[j] * rescale + functools.reduce(jnp.add, weights)
        acc_s[j] = acc_s[j] * rescale + jnp.dot(probs, vals, preferred_element_type=F32)
        m_s[j] = new

    def column_bias(n, limit):
        return jnp.where(lax.broadcasted_iota(jnp.int32, (1, n), 1) < limit, 0.0, NEG).astype(F32)

    def absorb_column(j, xx, first, planes):
        n = planes * 2 * KEEP
        own = jnp.where(xx < x, 2 * KEEP, jnp.where(xx == x, c * KEEP, 0))
        limit = z * 2 * KEEP + own - first * 2 * KEEP
        kv = kvbuf[pl.ds(slot_of(xx, first, 0), 2 * planes)].reshape(n, 2 * HD)
        absorb(j, kv, column_bias(n, limit))

    def each_chunk(body):
        lax.fori_loop(0, NCH, lambda j, carry: (body(j), carry)[1], 0, unroll=2)

    def local(j):
        row = lax.broadcasted_iota(jnp.int32, (QROWS, BLK), 0) % ROWS
        row = (row // 16) * 64 + j * 16 + row % 16
        key = lax.broadcasted_iota(jnp.int32, (QROWS, BLK), 1)
        absorb(j, kvown[...], jnp.where(key <= row, 0.0, NEG).astype(F32))

    each_chunk(local)

    arrivals = {
        0: ((event_column, 1),),
        1: ((event_column, 2), (event_column, 3), (event_sides, 0), (event_sides, 1)),
        2: ((event_opposite, 0), (event_opposite, 1)),
        3: ((event_sides, 2),),
    }

    def half_column(i, carry):
        for at, due in arrivals.items():

            @pl.when(i == at)
            def _():
                for what, turn in due:
                    event(what, turn)

        d = jnp.where(i == 0, 0, jnp.where(i == 1, 3, i - 1))

        @pl.when((z >= 2) | (i == 0))
        def _():
            event(event_sibling, 0, d)
            event(event_sibling, 1, d)
            first = z // 2 * 2
            each_chunk(lambda j: absorb_column(j, (x + d) % NX, first, 2))

        return carry

    lax.fori_loop(0, 4, half_column, 0)
    event(event_opposite, 2)
    event(event_sides, 3)

    def x_move(j, d):
        ref = xbuf.at[y, j]
        return remote(ref, ref, x_send.at[d - 1, j], x_recv.at[d - 1, j], (h, at_y(d)))

    def x_wait(j, d):
        ref = xbuf.at[(y + NY - d) % NY, j]
        remote(ref, ref, x_send.at[d - 1, j], x_recv.at[d - 1, j], (h, at_y(d))).wait_recv()

    def z_move(j):
        return remote(ysend.at[j], zbuf.at[j], z_send.at[j], z_recv.at[j], (h, other))

    def o_move(j, d):
        to = (y + d) % NY
        return remote(
            fbuf.at[j, pl.ds(to * 16, 16), :],
            out_ref.at[pl.ds(j * 16, 16), pl.ds(y * COLS, COLS)],
            o_send.at[d - 1, j], o_recv.at[d - 1, j], (h, at_y(d)),
        )

    def o_wait(j, d):
        src = (y + NY - d) % NY
        ref = out_ref.at[pl.ds(j * 16, 16), pl.ds(src * COLS, COLS)]
        remote(ref, ref, o_send.at[d - 1, j], o_recv.at[d - 1, j], (h, at_y(d))).wait_recv()

    def attend(j):
        def one(i, carry):
            d = jnp.where(i == 0, 0, jnp.where(i == 1, 3, i - 1))

            @pl.when(j == 0)
            def _():
                pl.when((i == 3) & (z >= 3))(lambda: event_opposite(3))
                turn = jnp.where(z >= 2, 2, 0)
                event(event_sibling, turn, d)
                event(event_sibling, turn + 1, d)

            absorb_column(j, (x + d) % NX, 0, 2)
            return carry

        lax.fori_loop(jnp.where(z >= 2, 0, 1), 4, one, 0)
        absorb(j, kvbuf[ANCHOR], column_bias(KEEP, jnp.where(h > 0, alen_ref[0], 0)))
        total = jnp.sum(l_s[j], axis=1, keepdims=True)
        attended = (acc_s[j] / total).astype(BF16)
        for i in range(QPG):
            xbuf[y, j, :, i * HD : (i + 1) * HD] = attended[i * ROWS : (i + 1) * ROWS]
        for d in (1, 3, 2):
            x_move(j, d).start()

        @pl.when(j == 1)
        def _():
            w_local.wait()
            for d in (1, 2, 3):
                w_in(d).wait_recv()
                w_pass(d, c).start()

    def project(j):
        @pl.when(j == 0)
        def _():
            for d in (1, 2, 3):
                w_pass(d, 1 - c).wait_recv()

        for d in (1, 2, 3):
            x_wait(j, d)
        ysc[...] = functools.reduce(
            jnp.add,
            [jnp.dot(xbuf[i, j], wbuf[i], preferred_element_type=F32) for i in range(NY)],
        )
        mine = ROWS // 2
        ysend[j] = ysc[pl.ds((1 - zh) * mine, mine), :].astype(BF16)
        z_move(j).start()
        yown[j] = ysc[pl.ds(zh * mine, mine), :]

    def finish(j):
        z_move(j).wait_recv()
        fbuf[j] = (yown[j] + zbuf[j].astype(F32)).astype(BF16)
        for d in (1, 2, 3):
            o_move(j, d).start()
        out_ref[pl.ds(j * 16, 16), pl.ds(y * COLS, COLS)] = fbuf[j, pl.ds(y * 16, 16), :]

    def tail(step, carry):
        for lag, stage in ((0, attend), (2, project), (3, finish)):
            j = step - lag
            pl.when((j >= 0) & (j < NCH))(functools.partial(stage, j))
        return carry

    lax.fori_loop(0, NCH + 3, tail, 0)

    for d in (1, 2, 3):
        w_out(d).wait_send()
        w_pass(d, c).wait_send()

    upward(sent)

    def drain(turn, carry):
        sideways(turn, sent)
        for d in (1, 2, 3):
            across(d, turn, sent)
        return carry

    lax.fori_loop(0, z + 1, drain, 0)

    def drain_tail(j, carry):
        z_move(j).wait_send()
        for d in (1, 2, 3):
            x_move(j, d).wait_send()
            o_move(j, d).wait_send()
            o_wait(j, d)
        return carry

    lax.fori_loop(0, NCH, drain_tail, 0)


def on_device(queries, keys, values, out_weight, keep, anchor_len):
    vmem, dma = pltpu.VMEM, pltpu.SemaphoreType.DMA
    mine = ROWS // 2
    return pl.pallas_call(
        kernel,
        out_shape=jax.ShapeDtypeStruct((BLK // 8, 4 * COLS), BF16),
        in_specs=[pl.BlockSpec(memory_space=pl.ANY)] * 6,
        out_specs=pl.BlockSpec(memory_space=pltpu.VMEM),
        scratch_shapes=[
            vmem((8, BLK // 8, QPG * HD), BF16),
            vmem((1, KEEP), jnp.int32),
            pltpu.SMEM((1,), jnp.int32),
            dma((5,)),
            vmem((BLK, 2 * HD), BF16),
            vmem((NZ * PLANE + 1, KEEP, 2 * HD), BF16),
            vmem((NCH, QROWS, 2 * HD), BF16),
            vmem((NCH, QROWS, HD), F32),
            vmem((NCH, QROWS, HD), F32),
            vmem((NCH, QROWS, HD), F32),
            vmem((NY, NCH, ROWS, QPG * HD), BF16),
            vmem((NY, BLK, COLS), BF16),
            vmem((ROWS, COLS), F32),
            vmem((NCH, mine, COLS), F32),
            vmem((NCH, mine, COLS), BF16),
            vmem((NCH, mine, COLS), BF16),
            vmem((NCH, mine, COLS), BF16),
            dma((8, NZ + 3)),
            dma((NZ * PLANE + 1,)),
            dma((3,)),
            dma((3,)),
            dma((3,)),
            dma((3,)),
            dma,
            dma((3, NCH)),
            dma((3, NCH)),
            dma((NCH,)),
            dma((NCH,)),
            dma((3, NCH)),
            dma((3, NCH)),
        ],
        compiler_params=pltpu.CompilerParams(
            collective_id=0, has_side_effects=True, vmem_limit_bytes=60 * 2**20
        ),
        cost_estimate=pl.CostEstimate(
            flops=11 * 10**9, bytes_accessed=7 * 10**6, transcendentals=18 * 10**6
        ),
    )(
        queries.reshape(8, BLK // 8, QPG * HD),
        keys,
        values,
        keep.reshape(1, KEEP),
        anchor_len,
        out_weight,
    )


def solution(mesh):
    placed = (
        P("hst", "kv"),
        P("hst", "kv"),
        P("hst", "kv"),
        P("kv", None),
        P("hst", "kv", None),
        P("kv"),
    )
    return jax.shard_map(
        on_device, mesh=mesh, in_specs=placed, out_specs=P(("hst", "kv"), None), check_vma=False
    )
```

```python
import functools
import math

import jax
import jax.numpy as jnp
from jax import lax
from jax.experimental import pallas as pl
from jax.experimental.pallas import tpu as pltpu
from jax.sharding import PartitionSpec as P

HD = 128
QPG = 4
BLK = 512
KEEP = 256
NX, NZ, NY = 4, 4, 4
PLANE = 2 * NX
ANCHOR = NZ * PLANE
NCH = 4
ROWS = BLK // NCH
QROWS = QPG * ROWS
COLS = 1024
SCALE = math.log2(math.e) / math.sqrt(HD)
NEG = -1e30
F32, BF16 = jnp.float32, jnp.bfloat16
MESH = pl.DeviceIdType.MESH


def kernel(
    q_hbm, k_hbm, v_hbm, keep_hbm, alen_hbm, w_ref, out_ref,
    q_ref, keep_ref, alen_ref, in_sem,
    kvown, kvbuf, qs, m_s, l_s, acc_s, xbuf, wbuf, ysc, yown, ysend, zbuf, fbuf,
    kv_send, kv_recv, w_send, w_recv, wl_send, wl_recv, w_own,
    x_send, x_recv, z_send, z_recv, o_send, o_recv,
):
    h = lax.axis_index("hst")
    g = lax.axis_index("kv")
    z, x, c = h // PLANE, (h % PLANE) // 2, h % 2
    zh, y = g // NY, g % NY
    sib = z * PLANE + 2 * x + (1 - c)
    other = (1 - zh) * NY + y

    def at_x(d):
        return z * PLANE + 2 * ((x + d) % NX) + c

    def at_y(d):
        return zh * NY + (y + d) % NY

    def remote(src, dst, send, recv, device):
        return pltpu.make_async_remote_copy(
            src_ref=src, dst_ref=dst, send_sem=send, recv_sem=recv,
            device_id=device, device_id_type=MESH,
        )

    def start(copy):
        copy.start()

    def sent(copy):
        copy.wait_send()

    barrier = pltpu.get_barrier_semaphore()
    partners = [(sib, g), (h, other)]
    for d in (1, 2, 3):
        partners += [(at_x(d), g), (h, at_y(d)), ((h + d * PLANE) % (NZ * PLANE), g)]
    for device in partners:
        pl.semaphore_signal(barrier, inc=1, device_id=device, device_id_type=MESH)

    loads = [
        pltpu.make_async_copy(src, dst, in_sem.at[i])
        for i, (src, dst) in enumerate(
            [
                (k_hbm, kvown.at[:, pl.ds(0, HD)]),
                (v_hbm, kvown.at[:, pl.ds(HD, HD)]),
                (keep_hbm, keep_ref),
                (q_hbm, q_ref),
                (alen_hbm, alen_ref),
            ]
        )
    ]
    for copy in loads:
        copy.start()
    for copy in loads[:3]:
        copy.wait()

    def slot_of(xx, plane, core):
        return xx * 2 * NZ + plane * 2 + core

    positions = lax.broadcasted_iota(jnp.int32, (BLK, KEEP), 0)
    onehot = (positions == keep_ref[...]).astype(F32).astype(BF16)
    kvbuf[slot_of(x, z, c)] = lax.dot_general(
        onehot, kvown[...], (((0,), (0,)), ((), ())), preferred_element_type=F32
    ).astype(BF16)

    @pl.when(h == 0)
    def _():
        kvbuf[ANCHOR] = kvown[:KEEP, :]

    pl.semaphore_wait(barrier, len(partners))

    half = BLK // 2

    def w_out(d):
        dst = (y + d) % NY
        return remote(
            w_ref.at[pl.ds(c * half, half), pl.ds(dst * COLS, COLS)],
            wbuf.at[y, pl.ds(c * half, half), :],
            w_send.at[d - 1], w_recv.at[d - 1], (h, at_y(d)),
        )

    def w_in(d):
        src = (y + NY - d) % NY
        ref = wbuf.at[src, pl.ds(c * half, half), :]
        return remote(ref, ref, w_send.at[d - 1], w_recv.at[d - 1], (h, at_y(NY - d)))

    def w_pass(d, core):
        src = (y + NY - d) % NY
        ref = wbuf.at[src, pl.ds(core * half, half), :]
        return remote(ref, ref, wl_send.at[d - 1], wl_recv.at[d - 1], (sib, g))

    w_local = pltpu.make_async_copy(w_ref.at[:, pl.ds(y * COLS, COLS)], wbuf.at[y], w_own)

    def kv_move(slot, device, kind, turn, act):
        ref = kvbuf.at[slot]
        act(remote(ref, ref, kv_send.at[kind, turn], kv_recv.at[slot], (device, g)))

        @pl.when(slot == 0)
        def _():
            anchor = kvbuf.at[ANCHOR]
            at = NZ + turn if kind == 0 else NZ
            act(remote(anchor, anchor, kv_send.at[kind, at], kv_recv.at[ANCHOR], (device, g)))

    def kv_wait(xx, plane, core):
        kv_move(slot_of(xx, plane, core), sib, 0, 0, lambda copy: copy.wait_recv())

    def upward(act):
        for d in (1, 2, 3):

            @pl.when(z + d < NZ)
            def _():
                kv_move(slot_of(x, z, c), h + d * PLANE, 0, d - 1, act)

    def sideways(turn, act):
        plane = z - turn
        slot = slot_of(x, plane, c)
        kv_move(slot, at_x(1), 1, plane, act)
        kv_move(slot, at_x(3), 2, plane, act)
        kv_move(slot, sib, 3, plane, act)
        kv_move(slot, at_x(2), 4, plane, act)

    def across(d, turn, act):
        plane = z - turn
        kv_move(slot_of((x + d) % NX, plane, c), sib, 4 + d, plane, act)

    def event_column(turn):
        kv_wait(x, z - turn, c)
        sideways(turn, start)

    def event_sides(turn):
        for d in (3, 1):
            kv_wait((x + d) % NX, z - turn, c)
            across(d, turn, start)

    def event_opposite(turn):
        kv_wait((x + 2) % NX, z - turn, c)
        across(2, turn, start)

    def event_sibling(d, turn):
        kv_wait((x + d) % NX, z - turn, 1 - c)

    def event(what, turn, *args):
        pl.when(z >= turn)(lambda: what(*args, turn))

    upward(start)
    sideways(0, start)
    w_local.start()
    for d in (1, 2, 3):
        w_out(d).start()

    @pl.when(z % 2 == 0)
    def _():
        def clear(xx, carry):
            kvbuf[pl.ds(slot_of(xx, z + 1, 0), 2)] = jnp.zeros((2, KEEP, 2 * HD), BF16)
            return carry

        lax.fori_loop(0, NX, clear, 0)

    for copy in loads[3:]:
        copy.wait()

    def prepare(j, carry):
        for i in range(QPG):
            rows = q_ref[:, pl.ds(j * 16, 16), i * HD : (i + 1) * HD]
            scaled = rows.reshape(ROWS, HD).astype(F32) * SCALE
            high = scaled.astype(BF16)
            qs[j, i * ROWS : (i + 1) * ROWS, :HD] = high
            qs[j, i * ROWS : (i + 1) * ROWS, HD:] = (scaled - high.astype(F32)).astype(BF16)
        m_s[j] = jnp.full((QROWS, HD), NEG, F32)
        l_s[j] = jnp.zeros((QROWS, HD), F32)
        acc_s[j] = jnp.zeros((QROWS, HD), F32)
        return carry

    lax.fori_loop(0, NCH, prepare, 0)

    def absorb(j, kv, bias):
        keys, vals = kv[:, :HD], kv[:, HD:]
        tiles = [slice(i * HD, (i + 1) * HD) for i in range(kv.shape[0] // HD)]
        scores = lax.dot_general(
            qs[j], jnp.concatenate([keys, keys], axis=1), (((1,), (1,)), ((), ())),
            preferred_element_type=F32,
        )
        scores = scores + bias
        top = functools.reduce(jnp.maximum, [scores[:, t] for t in tiles])
        old = m_s[j]
        new = jnp.maximum(old, jnp.max(top, axis=1, keepdims=True))
        rescale = jnp.exp2(old - new)
        weights = [jnp.exp2(scores[:, t] - new) for t in tiles]
        probs = jnp.concatenate([w.astype(BF16) for w in weights], axis=1)
        l_s[j] = l_s[j] * rescale + functools.reduce(jnp.add, weights)
        acc_s[j] = acc_s[j] * rescale + jnp.dot(probs, vals, preferred_element_type=F32)
        m_s[j] = new

    def column_bias(n, limit):
        return jnp.where(lax.broadcasted_iota(jnp.int32, (1, n), 1) < limit, 0.0, NEG).astype(F32)

    def absorb_column(j, xx, first, planes):
        n = planes * 2 * KEEP
        own = jnp.where(xx < x, 2 * KEEP, jnp.where(xx == x, c * KEEP, 0))
        limit = z * 2 * KEEP + own - first * 2 * KEEP
        kv = kvbuf[pl.ds(slot_of(xx, first, 0), 2 * planes)].reshape(n, 2 * HD)
        absorb(j, kv, column_bias(n, limit))

    def each_chunk(body):
        lax.fori_loop(0, NCH, lambda j, carry: (body(j), carry)[1], 0, unroll=2)

    def local(j):
        row = lax.broadcasted_iota(jnp.int32, (QROWS, BLK), 0) % ROWS
        row = (row // 16) * 64 + j * 16 + row % 16
        key = lax.broadcasted_iota(jnp.int32, (QROWS, BLK), 1)
        absorb(j, kvown[...], jnp.where(key <= row, 0.0, NEG).astype(F32))

    each_chunk(local)

    arrivals = {
        0: ((event_column, 1),),
        1: ((event_column, 2), (event_column, 3), (event_sides, 0), (event_sides, 1)),
        2: ((event_opposite, 0), (event_opposite, 1)),
        3: ((event_sides, 2),),
    }

    def half_column(i, carry):
        for at, due in arrivals.items():

            @pl.when(i == at)
            def _():
                for what, turn in due:
                    event(what, turn)

        d = jnp.where(i == 0, 0, jnp.where(i == 1, 3, i - 1))

        @pl.when((z >= 2) | (i == 0))
        def _():
            event(event_sibling, 0, d)
            event(event_sibling, 1, d)
            first = z // 2 * 2
            each_chunk(lambda j: absorb_column(j, (x + d) % NX, first, 2))

        return carry

    lax.fori_loop(0, 4, half_column, 0)
    event(event_opposite, 2)
    event(event_sides, 3)

    def x_move(j, d):
        ref = xbuf.at[y, j]
        return remote(ref, ref, x_send.at[d - 1, j], x_recv.at[d - 1, j], (h, at_y(d)))

    def x_wait(j, d):
        ref = xbuf.at[(y + NY - d) % NY, j]
        remote(ref, ref, x_send.at[d - 1, j], x_recv.at[d - 1, j], (h, at_y(d))).wait_recv()

    def z_move(j):
        return remote(ysend.at[j], zbuf.at[j], z_send.at[j], z_recv.at[j], (h, other))

    def o_move(j, d):
        to = (y + d) % NY
        return remote(
            fbuf.at[j, pl.ds(to * 16, 16), :],
            out_ref.at[pl.ds(j * 16, 16), pl.ds(y * COLS, COLS)],
            o_send.at[d - 1, j], o_recv.at[d - 1, j], (h, at_y(d)),
        )

    def o_wait(j, d):
        src = (y + NY - d) % NY
        ref = out_ref.at[pl.ds(j * 16, 16), pl.ds(src * COLS, COLS)]
        remote(ref, ref, o_send.at[d - 1, j], o_recv.at[d - 1, j], (h, at_y(d))).wait_recv()

    def attend(j):
        def one(i, carry):
            d = jnp.where(i == 0, 0, jnp.where(i == 1, 3, i - 1))

            @pl.when(j == 0)
            def _():
                pl.when((i == 2) & (z >= 3))(lambda: event_opposite(3))
                turn = jnp.where(z >= 2, 2, 0)
                event(event_sibling, turn, d)
                event(event_sibling, turn + 1, d)

            absorb_column(j, (x + d) % NX, 0, 2)
            return carry

        lax.fori_loop(jnp.where(z >= 2, 0, 1), 4, one, 0)
        absorb(j, kvbuf[ANCHOR], column_bias(KEEP, jnp.where(h > 0, alen_ref[0], 0)))
        total = jnp.sum(l_s[j], axis=1, keepdims=True)
        attended = (acc_s[j] / total).astype(BF16)
        for i in range(QPG):
            xbuf[y, j, :, i * HD : (i + 1) * HD] = attended[i * ROWS : (i + 1) * ROWS]
        for d in (1, 3, 2):
            x_move(j, d).start()

        @pl.when(j == 1)
        def _():
            w_local.wait()
            for d in (1, 2, 3):
                w_in(d).wait_recv()
                w_pass(d, c).start()

    def project(j):
        @pl.when(j == 0)
        def _():
            for d in (1, 2, 3):
                w_pass(d, 1 - c).wait_recv()

        for d in (1, 2, 3):
            x_wait(j, d)
        ysc[...] = functools.reduce(
            jnp.add,
            [jnp.dot(xbuf[i, j], wbuf[i], preferred_element_type=F32) for i in range(NY)],
        )
        mine = ROWS // 2
        ysend[j] = ysc[pl.ds((1 - zh) * mine, mine), :].astype(BF16)
        z_move(j).start()
        yown[j] = ysc[pl.ds(zh * mine, mine), :]

    def finish(j):
        z_move(j).wait_recv()
        fbuf[j] = (yown[j] + zbuf[j].astype(F32)).astype(BF16)
        for d in (1, 2, 3):
            o_move(j, d).start()
        out_ref[pl.ds(j * 16, 16), pl.ds(y * COLS, COLS)] = fbuf[j, pl.ds(y * 16, 16), :]

    def tail(step, carry):
        for lag, stage in ((0, attend), (2, project), (3, finish)):
            j = step - lag
            pl.when((j >= 0) & (j < NCH))(functools.partial(stage, j))
        return carry

    lax.fori_loop(0, NCH + 3, tail, 0)

    for d in (1, 2, 3):
        w_out(d).wait_send()
        w_pass(d, c).wait_send()

    upward(sent)

    def drain(turn, carry):
        sideways(turn, sent)
        for d in (1, 2, 3):
            across(d, turn, sent)
        return carry

    lax.fori_loop(0, z + 1, drain, 0)

    def drain_tail(j, carry):
        z_move(j).wait_send()
        for d in (1, 2, 3):
            x_move(j, d).wait_send()
            o_move(j, d).wait_send()
            o_wait(j, d)
        return carry

    lax.fori_loop(0, NCH, drain_tail, 0)


def on_device(queries, keys, values, out_weight, keep, anchor_len):
    vmem, dma = pltpu.VMEM, pltpu.SemaphoreType.DMA
    mine = ROWS // 2
    return pl.pallas_call(
        kernel,
        out_shape=jax.ShapeDtypeStruct((BLK // 8, 4 * COLS), BF16),
        in_specs=[pl.BlockSpec(memory_space=pl.ANY)] * 6,
        out_specs=pl.BlockSpec(memory_space=pltpu.VMEM),
        scratch_shapes=[
            vmem((8, BLK // 8, QPG * HD), BF16),
            vmem((1, KEEP), jnp.int32),
            pltpu.SMEM((1,), jnp.int32),
            dma((5,)),
            vmem((BLK, 2 * HD), BF16),
            vmem((NZ * PLANE + 1, KEEP, 2 * HD), BF16),
            vmem((NCH, QROWS, 2 * HD), BF16),
            vmem((NCH, QROWS, HD), F32),
            vmem((NCH, QROWS, HD), F32),
            vmem((NCH, QROWS, HD), F32),
            vmem((NY, NCH, ROWS, QPG * HD), BF16),
            vmem((NY, BLK, COLS), BF16),
            vmem((ROWS, COLS), F32),
            vmem((NCH, mine, COLS), F32),
            vmem((NCH, mine, COLS), BF16),
            vmem((NCH, mine, COLS), BF16),
            vmem((NCH, mine, COLS), BF16),
            dma((8, NZ + 3)),
            dma((NZ * PLANE + 1,)),
            dma((3,)),
            dma((3,)),
            dma((3,)),
            dma((3,)),
            dma,
            dma((3, NCH)),
            dma((3, NCH)),
            dma((NCH,)),
            dma((NCH,)),
            dma((3, NCH)),
            dma((3, NCH)),
        ],
        compiler_params=pltpu.CompilerParams(
            collective_id=0, has_side_effects=True, vmem_limit_bytes=60 * 2**20
        ),
        cost_estimate=pl.CostEstimate(
            flops=11 * 10**9, bytes_accessed=7 * 10**6, transcendentals=18 * 10**6
        ),
    )(
        queries.reshape(8, BLK // 8, QPG * HD),
        keys,
        values,
        keep.reshape(1, KEEP),
        anchor_len,
        out_weight,
    )


def solution(mesh):
    placed = (
        P("hst", "kv"),
        P("hst", "kv"),
        P("hst", "kv"),
        P("kv", None),
        P("hst", "kv", None),
        P("kv"),
    )
    return jax.shard_map(
        on_device, mesh=mesh, in_specs=placed, out_specs=P(("hst", "kv"), None), check_vma=False
    )
```
